512 devices in a mesh: replica: 32 (over x, z_hi, y), fsdp: 16 (over z_lo, core).
Axes of the slice: x: 4, y: 4, z: 16 (z_hi: 2, z_lo: 8; z = z_hi * 8 + z_lo), core: 2. Of those that a mesh axis runs over, the one named last changes fastest.
Arguments:
- features: bfloat16 [32, 3072, 2048], P('replica', 'fsdp'), may hold values from -6 to 6
- cotangent: bfloat16 [32, 3072, 2048], P('replica', 'fsdp'), may hold values from -6 to 6
- master: float32 [32, 2048, 2048], P('replica', None, 'fsdp'), may hold values from -0.75 to 0.75
- moment: bfloat16 [32, 2048, 2048], P('replica', None, 'fsdp'), may hold values from -6 to 6
- variance: float32 [32, 2048, 2048], P('replica', None, 'fsdp'), may hold values from 0.05 to 1
- step_count: int32 [1], replicated, may hold values from 1 to 24
Outputs:
- mixed: float32 [32, 2048, 2048], P('replica', None, 'fsdp')
The draws below stay inside these ranges and needn't reach their ends.
All inputs are finite; a program needn't handle non-finite values.
Results may differ from the reference program's by a relative error of at most 0.0022.
Values may be sent and summed in bfloat16 or wider, within the bound.
No kernel may reach another device: no remote copies, remote signals or barrier semaphores. Data moves between devices by JAX's collectives and lax.ppermute only.
A program may use at most 64 MiB of HBM per device.

```python
import math
import jax
import jax.numpy as jnp
from jax import lax

D_IN = 2048
HEADS = 16
HEAD = 128
E = 2048
TOKENS = 3072
REPLICAS = 32


def block_levels(rng, shape, split, low, top_value):
    gain = 1.0
    for axis_at, parts in split:
        heights = jax.random.uniform(jax.random.fold_in(jax.random.fold_in(rng, 6), axis_at), (parts,), jnp.float32, low / len(split), top_value / len(split))
        gain = gain * jnp.repeat(jnp.exp(heights), shape[axis_at] // parts).reshape((-1,) + (1,) * (len(shape) - 1 - axis_at))
    return gain


def scatter_about(own_key, dims, spread, limit, shards=(), held_as=jnp.bfloat16):
    drawn = spread * jax.random.normal(own_key, dims, jnp.float32)
    if shards:
        drawn = drawn * block_levels(own_key, dims, shards, -0.22, 0.18)
    return jnp.clip(drawn, -limit, limit).astype(held_as)


def setup_inputs(seed: int = 0) -> dict:
    splits = jax.random.split(jax.random.key(seed), 7)
    features = scatter_about(splits[0], (REPLICAS, TOKENS, D_IN), 1.0, 6.0, ((0, 32), (1, 16)))
    cotangent = scatter_about(splits[1], (REPLICAS, TOKENS, E), 1.0, 6.0, ((0, 32), (1, 16)))
    master = scatter_about(splits[2], (REPLICAS, D_IN, E), 0.05, 0.75, ((0, 32), (2, 16)), jnp.float32)
    moment = scatter_about(splits[3], (REPLICAS, D_IN, E), 0.5, 6.0, ((0, 32), (2, 16)))
    variance = jnp.clip(jnp.exp(math.log(1.0) - 2.9957323 * jax.random.uniform(splits[4], (REPLICAS, D_IN, E), jnp.float32) ** block_levels(splits[4], (REPLICAS, D_IN, E), ((0, 32), (2, 16)), -0.2, 0.2)), 0.05, 1.0)
    step_count = jax.random.randint(splits[5], (1,), 1, 25).astype(jnp.int32)
    return {"features": features, "cotangent": cotangent, "master": master, "moment": moment, "variance": variance, "step_count": step_count}


def head_gradient(tokens, weights, cotangent, heads_here):
    scale = D_IN ** (-0.5)
    query = jnp.dot(tokens, weights, preferred_element_type=jnp.float32) * scale
    count_rows = query.shape[0]
    shaped = query.reshape(count_rows, heads_here, HEAD)
    inverse = lax.rsqrt(lax.optimization_barrier(jnp.mean(shaped * shaped, axis=-1, keepdims=True)) + 1e-06)
    normed = shaped * inverse
    upstream = cotangent.astype(jnp.float32).reshape(count_rows, heads_here, HEAD)
    projected = lax.optimization_barrier(jnp.mean(upstream * normed, axis=-1, keepdims=True))
    dquery = (inverse * (upstream - normed * projected)).reshape(count_rows, heads_here * HEAD).astype(jnp.bfloat16)
    return lax.dot_general(tokens, dquery, (((0,), (0,)), ((), ())), preferred_element_type=jnp.float32)

def reference(features, cotangent, master, moment, variance, step_count):

    def one_replica(packed):
        tokens, upstream, weight = packed
        return head_gradient(tokens, weight.astype(jnp.bfloat16), upstream, HEADS) * D_IN ** (-0.5)
    grads = lax.map(one_replica, (features, cotangent, master))
    counter = step_count[0]
    power = counter.astype(jnp.float32)
    correct_first = 1.0 - jnp.power(jnp.float32(0.9), power)
    correct_second = 1.0 - jnp.power(jnp.float32(0.999), power)
    first = 0.9 * moment.astype(jnp.float32) + 0.1 * grads
    second = 0.999 * variance + 0.001 * grads * grads
    update = 0.1 * (first / correct_first / (jnp.sqrt(second / correct_second) + 1e-08) + 0.1 * master)
    fresh = master - update
    distance = jnp.left_shift(jnp.int32(1), counter % 4)
    return 0.5 * (fresh + jnp.roll(fresh, distance, axis=0))
```

```python
from functools import partial

import jax
import jax.numpy as jnp
from jax import lax
from jax.experimental import pallas as pl
from jax.experimental.pallas import tpu as pltpu
from jax.sharding import PartitionSpec as P

D_IN = 2048
HEAD = 128
CORES = 2
ROWS = 512


def gradient_kernel(info, x_ref, w_ref, cot_ref, own_in, other_in, own_out, other_out):
    valid, block, core = info[0], info[1], info[2]

    @pl.when(valid > 0)
    def _():
        x = x_ref[...]
        query = jnp.dot(x, w_ref[...], preferred_element_type=jnp.float32) * D_IN ** (-0.5)
        cot = cot_ref[block].astype(jnp.float32)
        first, second = cot[:, :HEAD], cot[:, HEAD:]
        upstreams = (
            jnp.where(core == 0, first, second),
            jnp.where(core == 0, second, first),
        )
        parts = []
        for at, upstream in enumerate(upstreams):
            shaped = query[:, at * HEAD : (at + 1) * HEAD]
            inverse = lax.rsqrt(jnp.mean(shaped * shaped, axis=-1, keepdims=True) + 1e-06)
            normed = shaped * inverse
            projected = jnp.mean(upstream * normed, axis=-1, keepdims=True)
            parts.append((inverse * (upstream - normed * projected)).astype(jnp.bfloat16))
        dquery = jnp.concatenate(parts, axis=1)
        for at in range(0, D_IN, ROWS):
            rows = slice(at, at + ROWS)
            part = lax.dot_general(
                x_ref[:, rows], dquery, (((0,), (0,)), ((), ())), preferred_element_type=jnp.float32
            )
            own_out[rows, :] = own_in[rows, :] + part[:, :HEAD]
            other_out[rows, :] = other_in[rows, :] + part[:, HEAD:]


def accumulate(sums, x, weights, cots, valid, block, core):
    info = jnp.stack([valid, block, core]).astype(jnp.int32)
    vmem = pl.BlockSpec(memory_space=pltpu.VMEM)
    tokens = x.shape[0]
    return pl.pallas_call(
        gradient_kernel,
        out_shape=[jax.ShapeDtypeStruct(s.shape, s.dtype) for s in sums],
        in_specs=[pl.BlockSpec(memory_space=pltpu.SMEM)] + [vmem] * 5,
        out_specs=[vmem, vmem],
        input_output_aliases={4: 0, 5: 1},
        cost_estimate=pl.CostEstimate(
            flops=8 * tokens * D_IN * HEAD, bytes_accessed=6 * 2**20, transcendentals=2 * tokens
        ),
        compiler_params=pltpu.CompilerParams(vmem_limit_bytes=32 * 2**20),
    )(info, x, weights, cots, *sums)


def chip_pairs(chips, sources, step):
    return [
        (chip * CORES + core, (chip + step) * CORES + core)
        for chip in sources
        for core in range(CORES)
        if 0 <= chip + step < chips
    ]


def pull_fresh(value, distance):
    count = lax.axis_size("replica")
    pairs = [(source, (source + distance) % count) for source in range(count)]
    return lax.ppermute(value, "replica", pairs)


def body(features, cotangent, master, moment, variance, step_count):
    counter = step_count[0]
    selector = counter % 4
    params = master[0]
    tokens = features[0]
    devices = lax.axis_size("fsdp")
    chips = devices // CORES
    half = chips // 2
    index = lax.axis_index("fsdp")
    chip, core = index // CORES, index % CORES
    rows = tokens.shape[0]

    def hop(value, sources, step):
        return lax.ppermute(value, "fsdp", chip_pairs(chips, sources, step))

    groups = [[at * CORES + c for at in range(chips)] for c in range(CORES)]
    cots = lax.all_to_all(
        cotangent[0].reshape(rows, chips, CORES * HEAD).transpose(1, 0, 2),
        "fsdp",
        split_axis=0,
        concat_axis=0,
        axis_index_groups=groups,
    )
    weights = params.astype(jnp.bfloat16)
    swapped = [(at, at ^ 1) for at in range(devices)]
    weights = jnp.concatenate([weights, lax.ppermute(weights, "fsdp", swapped)], axis=1)

    arrived = [(tokens, jnp.int32(1), chip)]
    right = left = tokens
    for step in range(1, half + 1):
        right = hop(right, range(step - 1, chips), 1)
        left = hop(left, range(0, chips - step + 1), -1)
        if step < half:
            arrived.append((right, chip >= step, chip - step))
            arrived.append((left, chip < chips - step, chip + step))
    upper = chip >= half
    block = jnp.where(upper, right, left)
    for step in range(half, chips):
        if step > half:
            pairs = chip_pairs(chips, range(step - 1, chips), 1)
            pairs += chip_pairs(chips, range(0, chips - step + 1), -1)
            block = lax.ppermute(block, "fsdp", pairs)
        valid = jnp.where(upper, chip >= step, chip < chips - step)
        arrived.append((block, valid, jnp.where(upper, chip - step, chip + step)))

    sums = [jnp.zeros((D_IN, HEAD), jnp.float32)] * 2
    for x, valid, source in arrived:
        sums = accumulate(
            sums, x, weights, cots, valid, jnp.clip(source, 0, chips - 1), core
        )
    own, other = sums
    summed = own + lax.ppermute(other, "fsdp", swapped)

    grads = summed * D_IN ** (-0.5)
    power = counter.astype(jnp.float32)
    correct_first = 1.0 - jnp.power(jnp.float32(0.9), power)
    correct_second = 1.0 - jnp.power(jnp.float32(0.999), power)
    first = 0.9 * moment[0].astype(jnp.float32) + 0.1 * grads
    second = 0.999 * variance[0] + 0.001 * grads * grads
    update = 0.1 * (
        first / correct_first / (jnp.sqrt(second / correct_second) + 1e-08) + 0.1 * params
    )
    fresh = params - update
    received = lax.switch(
        selector,
        [partial(pull_fresh, distance=1 << level) for level in range(4)],
        fresh.astype(jnp.bfloat16),
    )
    return (0.5 * (fresh + received.astype(jnp.float32)))[None]


def solution(mesh):
    placed = (
        P("replica", "fsdp", None),
        P("replica", "fsdp", None),
        P("replica", None, "fsdp"),
        P("replica", None, "fsdp"),
        P("replica", None, "fsdp"),
        P(),
    )
    return jax.shard_map(
        body, mesh=mesh, in_specs=placed, out_specs=P("replica", None, "fsdp"), check_vma=False
    )
```

```python
from functools import partial

import jax
import jax.numpy as jnp
from jax import lax
from jax.experimental import pallas as pl
from jax.experimental.pallas import tpu as pltpu
from jax.sharding import PartitionSpec as P

D_IN = 2048
HEAD = 128
CORES = 2
ROWS = 512
PARTS = 2
WAYS = (1, -1)
EXCHANGE = 5


def gradient_kernel(info, *refs):
    xs, (w_ref, cot_ref, own_in, other_in, own_out, other_out) = refs[:PARTS], refs[PARTS:]
    valid, source, core = info[0], info[1], info[2]

    @pl.when(valid > 0)
    def _():
        x = jnp.concatenate([ref[...] for ref in xs], axis=0)
        query = jnp.dot(x, w_ref[...], preferred_element_type=jnp.float32) * D_IN ** (-0.5)
        cot = cot_ref[source].astype(jnp.float32)
        first, second = cot[:, :HEAD], cot[:, HEAD:]
        upstreams = (
            jnp.where(core == 0, first, second),
            jnp.where(core == 0, second, first),
        )
        parts = []
        for at, upstream in enumerate(upstreams):
            shaped = query[:, at * HEAD : (at + 1) * HEAD]
            inverse = lax.rsqrt(jnp.mean(shaped * shaped, axis=-1, keepdims=True) + 1e-06)
            normed = shaped * inverse
            projected = jnp.mean(upstream * normed, axis=-1, keepdims=True)
            parts.append((inverse * (upstream - normed * projected)).astype(jnp.bfloat16))
        dquery = jnp.concatenate(parts, axis=1)
        for at in range(0, D_IN, ROWS):
            rows = slice(at, at + ROWS)
            part = lax.dot_general(
                jnp.concatenate([ref[:, rows] for ref in xs], axis=0),
                dquery,
                (((0,), (0,)), ((), ())),
                preferred_element_type=jnp.float32,
            )
            own_out[rows, :] = own_in[rows, :] + part[:, :HEAD]
            other_out[rows, :] = other_in[rows, :] + part[:, HEAD:]


def accumulate(sums, weights, cots, core, xs, valid, source):
    source = jnp.clip(source, 0, cots.shape[0] - 1)
    info = jnp.stack([jnp.int32(valid), source, core])
    vmem = pl.BlockSpec(memory_space=pltpu.VMEM)
    tokens = cots.shape[1]
    return pl.pallas_call(
        gradient_kernel,
        out_shape=[jax.ShapeDtypeStruct(s.shape, s.dtype) for s in sums],
        in_specs=[pl.BlockSpec(memory_space=pltpu.SMEM)] + [vmem] * (PARTS + 4),
        out_specs=[vmem, vmem],
        input_output_aliases={PARTS + 3: 0, PARTS + 4: 1},
        cost_estimate=pl.CostEstimate(
            flops=8 * tokens * D_IN * HEAD, bytes_accessed=6 * 2**20, transcendentals=2 * tokens
        ),
        compiler_params=pltpu.CompilerParams(vmem_limit_bytes=32 * 2**20),
    )(info, *xs, weights, cots, *sums)


def pull_fresh(value, distance):
    count = lax.axis_size("replica")
    pairs = [(source, (source + distance) % count) for source in range(count)]
    return lax.ppermute(value, "replica", pairs)


def body(features, cotangent, master, moment, variance, step_count):
    counter = step_count[0]
    selector = counter % 4
    params = master[0]
    tokens = features[0]
    devices = lax.axis_size("fsdp")
    chips = devices // CORES
    half = chips // 2
    index = lax.axis_index("fsdp")
    chip, core = index // CORES, index % CORES
    rows = tokens.shape[0]

    groups = [[at * CORES + c for at in range(chips)] for c in range(CORES)]
    swapped = [(at, at ^ 1) for at in range(devices)]
    mine = params.astype(jnp.bfloat16)
    weights = jnp.concatenate([mine, lax.ppermute(mine, "fsdp", swapped)], axis=1)
    cots = cotangent[0].reshape(rows, chips, CORES * HEAD).transpose(1, 0, 2)

    def pairs_of(step, ways):
        pairs = []
        for core_at, way in enumerate(ways):
            sources = range(step - 1, chips) if way > 0 else range(0, chips - step + 1)
            pairs += [
                (at * CORES + core_at, (at + way) * CORES + core_at)
                for at in sources
                if 0 <= at + way < chips
            ]
        return pairs

    def hop(parts, pairs):
        return [lax.ppermute(part, "fsdp", pairs) for part in parts]

    def exchange(cots, *parts):
        cots, *parts = lax.optimization_barrier((cots, *parts))
        cots = lax.all_to_all(
            cots, "fsdp", split_axis=0, concat_axis=0, axis_index_groups=groups
        )
        return cots, parts

    upper = chip >= half
    parts = jnp.split(tokens, PARTS, axis=0)
    waiting = [(parts, 1, chip)]
    one, two = list(parts), list(parts)
    for step in range(1, half + 1):
        if step == EXCHANGE:
            cots, (one[0], two[0]) = exchange(cots, one[0], two[0])
        one, two = hop(one, pairs_of(step, WAYS)), hop(two, pairs_of(step, [-way for way in WAYS]))
        lead = (core == 0) | (WAYS[0] == WAYS[1])
        if step < half:
            for xs, first in ((list(one), lead), (list(two), ~lead)):
                valid = jnp.where(first, chip >= step, chip < chips - step)
                waiting.append((xs, valid, jnp.where(first, chip - step, chip + step)))
    block = [jnp.where(upper == lead, a, b) for a, b in zip(one, two)]
    for step in range(half, chips):
        if step > half:
            if step == EXCHANGE:
                cots, (block[0],) = exchange(cots, block[0])
            both = sorted(set(pairs_of(step, (1, 1)) + pairs_of(step, (-1, -1))))
            block = hop(block, both)
        valid = jnp.where(upper, chip >= step, chip < chips - step)
        waiting.append((list(block), valid, jnp.where(upper, chip - step, chip + step)))
    sums = tuple(jnp.zeros((D_IN, HEAD), jnp.float32) for _ in range(2))
    for xs, valid, source in waiting:
        sums = accumulate(sums, weights, cots, core, xs, valid, source)
    own, other = sums
    summed = own + lax.ppermute(other, "fsdp", swapped)

    grads = summed * D_IN ** (-0.5)
    power = counter.astype(jnp.float32)
    correct_first = 1.0 - jnp.power(jnp.float32(0.9), power)
    correct_second = 1.0 - jnp.power(jnp.float32(0.999), power)
    first = 0.9 * moment[0].astype(jnp.float32) + 0.1 * grads
    second = 0.999 * variance[0] + 0.001 * grads * grads
    update = 0.1 * (
        first / correct_first / (jnp.sqrt(second / correct_second) + 1e-08) + 0.1 * params
    )
    fresh = params - update
    received = lax.switch(
        selector,
        [partial(pull_fresh, distance=1 << level) for level in range(4)],
        fresh.astype(jnp.bfloat16),
    )
    return (0.5 * (fresh + received.astype(jnp.float32)))[None]


def solution(mesh):
    placed = (
        P("replica", "fsdp", None),
        P("replica", "fsdp", None),
        P("replica", None, "fsdp"),
        P("replica", None, "fsdp"),
        P("replica", None, "fsdp"),
        P(),
    )
    return jax.shard_map(
        body, mesh=mesh, in_specs=placed, out_specs=P("replica", None, "fsdp"), check_vma=False
    )
```

```python
from functools import partial

import jax
import jax.numpy as jnp
from jax import lax
from jax.experimental import pallas as pl
from jax.experimental.pallas import tpu as pltpu
from jax.sharding import PartitionSpec as P

D_IN = 2048
HEAD = 128
CORES = 2
LINES = 4
ROWS = 512
PARTS = 2
WAYS = (1, -1)
EXCHANGE = 5


def gradient_kernel(info, *refs):
    xs, (w_ref, cot_ref, own_in, other_in, own_out, other_out) = refs[:PARTS], refs[PARTS:]
    valid, source, core = info[0], info[1], info[2]

    @pl.when(valid > 0)
    def _():
        x = jnp.concatenate([ref[...] for ref in xs], axis=0)
        query = jnp.dot(x, w_ref[...], preferred_element_type=jnp.float32) * D_IN ** (-0.5)
        cot = cot_ref[source].astype(jnp.float32)
        first, second = cot[:, :HEAD], cot[:, HEAD:]
        upstreams = (
            jnp.where(core == 0, first, second),
            jnp.where(core == 0, second, first),
        )
        parts = []
        for at, upstream in enumerate(upstreams):
            shaped = query[:, at * HEAD : (at + 1) * HEAD]
            inverse = lax.rsqrt(jnp.mean(shaped * shaped, axis=-1, keepdims=True) + 1e-06)
            normed = shaped * inverse
            projected = jnp.mean(upstream * normed, axis=-1, keepdims=True)
            parts.append((inverse * (upstream - normed * projected)).astype(jnp.bfloat16))
        dquery = jnp.concatenate(parts, axis=1)
        for at in range(0, D_IN, ROWS):
            rows = slice(at, at + ROWS)
            part = lax.dot_general(
                jnp.concatenate([ref[:, rows] for ref in xs], axis=0),
                dquery,
                (((0,), (0,)), ((), ())),
                preferred_element_type=jnp.float32,
            )
            own_out[rows, :] = own_in[rows, :] + part[:, :HEAD]
            other_out[rows, :] = other_in[rows, :] + part[:, HEAD:]


def accumulate(sums, weights, cots, core, xs, valid, source):
    source = jnp.clip(source, 0, cots.shape[0] - 1)
    info = jnp.stack([jnp.int32(valid), source, core])
    vmem = pl.BlockSpec(memory_space=pltpu.VMEM)
    tokens = cots.shape[1]
    return pl.pallas_call(
        gradient_kernel,
        out_shape=[jax.ShapeDtypeStruct(s.shape, s.dtype) for s in sums],
        in_specs=[pl.BlockSpec(memory_space=pltpu.SMEM)] + [vmem] * (PARTS + 4),
        out_specs=[vmem, vmem],
        input_output_aliases={PARTS + 3: 0, PARTS + 4: 1},
        cost_estimate=pl.CostEstimate(
            flops=8 * tokens * D_IN * HEAD, bytes_accessed=6 * 2**20, transcendentals=2 * tokens
        ),
        compiler_params=pltpu.CompilerParams(vmem_limit_bytes=32 * 2**20),
    )(info, *xs, weights, cots, *sums)


def pull_fresh(value, distance):
    count = lax.axis_size("replica")
    if distance >= LINES:
        pairs = [(source, (source + distance) % count) for source in range(count)]
        return lax.ppermute(value, "replica", pairs)

    groups = range(0, count, LINES)
    line = lax.axis_index("replica") % LINES
    leaving = range(LINES - distance, LINES)
    lanes = LINES // distance
    slices = jnp.split(value, lanes)
    near = [(g + y, g + y + distance) for g in groups for y in range(LINES - distance)]
    held = []
    for k, part in enumerate(slices[:-1]):
        held.append(
            lax.ppermute(
                part,
                "replica",
                [(g + y, g + (y + distance * (k + 1)) % LINES) for g in groups for y in leaving],
            )
        )
    held.append(slices[-1])
    direct = lax.ppermute(value, "replica", near)
    far = []
    for k, part in enumerate(held):
        way = [
            (g + (y + distance * (k + 1)) % LINES, (g + y + distance) % count)
            for g in groups
            for y in leaving
        ]
        far.append(lax.ppermute(part, "replica", way))
    return jnp.where(line < distance, jnp.concatenate(far), direct)


def body(features, cotangent, master, moment, variance, step_count):
    counter = step_count[0]
    selector = counter % 4
    params = master[0]
    tokens = features[0]
    devices = lax.axis_size("fsdp")
    chips = devices // CORES
    half = chips // 2
    index = lax.axis_index("fsdp")
    chip, core = index // CORES, index % CORES
    rows = tokens.shape[0]

    groups = [[at * CORES + c for at in range(chips)] for c in range(CORES)]
    swapped = [(at, at ^ 1) for at in range(devices)]
    mine = params.astype(jnp.bfloat16)
    weights = jnp.concatenate([mine, lax.ppermute(mine, "fsdp", swapped)], axis=1)
    cots = cotangent[0].reshape(rows, chips, CORES * HEAD).transpose(1, 0, 2)

    def pairs_of(step, ways):
        pairs = []
        for core_at, way in enumerate(ways):
            sources = range(step - 1, chips) if way > 0 else range(0, chips - step + 1)
            pairs += [
                (at * CORES + core_at, (at + way) * CORES + core_at)
                for at in sources
                if 0 <= at + way < chips
            ]
        return pairs

    def hop(parts, pairs):
        return [lax.ppermute(part, "fsdp", pairs) for part in parts]

    def exchange(cots, *parts):
        cots, *parts = lax.optimization_barrier((cots, *parts))
        cots = lax.all_to_all(
            cots, "fsdp", split_axis=0, concat_axis=0, axis_index_groups=groups
        )
        return cots, parts

    upper = chip >= half
    parts = jnp.split(tokens, PARTS, axis=0)
    waiting = [(parts, 1, chip)]
    one, two = list(parts), list(parts)
    for step in range(1, half + 1):
        if step == EXCHANGE:
            cots, (one[0], two[0]) = exchange(cots, one[0], two[0])
        one, two = hop(one, pairs_of(step, WAYS)), hop(two, pairs_of(step, [-way for way in WAYS]))
        lead = (core == 0) | (WAYS[0] == WAYS[1])
        if step < half:
            for xs, first in ((list(one), lead), (list(two), ~lead)):
                valid = jnp.where(first, chip >= step, chip < chips - step)
                waiting.append((xs, valid, jnp.where(first, chip - step, chip + step)))
    block = [jnp.where(upper == lead, a, b) for a, b in zip(one, two)]
    for step in range(half, chips):
        if step > half:
            if step == EXCHANGE:
                cots, (block[0],) = exchange(cots, block[0])
            both = sorted(set(pairs_of(step, (1, 1)) + pairs_of(step, (-1, -1))))
            block = hop(block, both)
        valid = jnp.where(upper, chip >= step, chip < chips - step)
        waiting.append((list(block), valid, jnp.where(upper, chip - step, chip + step)))
    sums = tuple(jnp.zeros((D_IN, HEAD), jnp.float32) for _ in range(2))
    for xs, valid, source in waiting:
        sums = accumulate(sums, weights, cots, core, xs, valid, source)
    own, other = sums
    summed = own + lax.ppermute(other, "fsdp", swapped)

    grads = summed * D_IN ** (-0.5)
    power = counter.astype(jnp.float32)
    correct_first = 1.0 - jnp.power(jnp.float32(0.9), power)
    correct_second = 1.0 - jnp.power(jnp.float32(0.999), power)
    first = 0.9 * moment[0].astype(jnp.float32) + 0.1 * grads
    second = 0.999 * variance[0] + 0.001 * grads * grads
    update = 0.1 * (
        first / correct_first / (jnp.sqrt(second / correct_second) + 1e-08) + 0.1 * params
    )
    fresh = params - update
    received = lax.switch(
        selector,
        [partial(pull_fresh, distance=1 << level) for level in range(4)],
        fresh.astype(jnp.bfloat16),
    )
    return (0.5 * (fresh + received.astype(jnp.float32)))[None]


def solution(mesh):
    placed = (
        P("replica", "fsdp", None),
        P("replica", "fsdp", None),
        P("replica", None, "fsdp"),
        P("replica", None, "fsdp"),
        P("replica", None, "fsdp"),
        P(),
    )
    return jax.shard_map(
        body, mesh=mesh, in_specs=placed, out_specs=P("replica", None, "fsdp"), check_vma=False
    )
```

```python
from functools import partial

import jax
import jax.numpy as jnp
from jax import lax
from jax.experimental import pallas as pl
from jax.experimental.pallas import tpu as pltpu
from jax.sharding import PartitionSpec as P

D_IN = 2048
HEAD = 128
CORES = 2
LINES = 4
OWN_LINE = {2: 1248, 4: 832}
ROWS = 512
PARTS = 2
WAYS = (1, -1)
EXCHANGE = 5


def gradient_kernel(info, *refs):
    xs, (w_ref, cot_ref, own_in, other_in, own_out, other_out) = refs[:PARTS], refs[PARTS:]
    valid, source, core = info[0], info[1], info[2]

    @pl.when(valid > 0)
    def _():
        x = jnp.concatenate([ref[...] for ref in xs], axis=0)
        query = jnp.dot(x, w_ref[...], preferred_element_type=jnp.float32) * D_IN ** (-0.5)
        cot = cot_ref[source].astype(jnp.float32)
        first, second = cot[:, :HEAD], cot[:, HEAD:]
        upstreams = (
            jnp.where(core == 0, first, second),
            jnp.where(core == 0, second, first),
        )
        parts = []
        for at, upstream in enumerate(upstreams):
            shaped = query[:, at * HEAD : (at + 1) * HEAD]
            inverse = lax.rsqrt(jnp.mean(shaped * shaped, axis=-1, keepdims=True) + 1e-06)
            normed = shaped * inverse
            projected = jnp.mean(upstream * normed, axis=-1, keepdims=True)
            parts.append((inverse * (upstream - normed * projected)).astype(jnp.bfloat16))
        dquery = jnp.concatenate(parts, axis=1)
        for at in range(0, D_IN, ROWS):
            rows = slice(at, at + ROWS)
            part = lax.dot_general(
                jnp.concatenate([ref[:, rows] for ref in xs], axis=0),
                dquery,
                (((0,), (0,)), ((), ())),
                preferred_element_type=jnp.float32,
            )
            own_out[rows, :] = own_in[rows, :] + part[:, :HEAD]
            other_out[rows, :] = other_in[rows, :] + part[:, HEAD:]


def accumulate(sums, weights, cots, core, xs, valid, source):
    source = jnp.clip(source, 0, cots.shape[0] - 1)
    info = jnp.stack([jnp.int32(valid), source, core])
    vmem = pl.BlockSpec(memory_space=pltpu.VMEM)
    tokens = cots.shape[1]
    return pl.pallas_call(
        gradient_kernel,
        out_shape=[jax.ShapeDtypeStruct(s.shape, s.dtype) for s in sums],
        in_specs=[pl.BlockSpec(memory_space=pltpu.SMEM)] + [vmem] * (PARTS + 4),
        out_specs=[vmem, vmem],
        input_output_aliases={PARTS + 3: 0, PARTS + 4: 1},
        cost_estimate=pl.CostEstimate(
            flops=8 * tokens * D_IN * HEAD, bytes_accessed=6 * 2**20, transcendentals=2 * tokens
        ),
        compiler_params=pltpu.CompilerParams(vmem_limit_bytes=32 * 2**20),
    )(info, *xs, weights, cots, *sums)


def pull_fresh(value, distance):
    count = lax.axis_size("replica")
    if distance >= LINES:
        pairs = [(source, (source + distance) % count) for source in range(count)]
        return lax.ppermute(value, "replica", pairs)

    groups = range(0, count, LINES)
    line = lax.axis_index("replica") % LINES
    leaving = range(LINES - distance, LINES)
    lanes = LINES // distance
    share = OWN_LINE[lanes]
    others = (value.shape[0] - share) // (lanes - 1) // 16 * 16
    slices = jnp.split(value, [others * k for k in range(1, lanes - 1)] + [value.shape[0] - share])
    near = [(g + y, g + y + distance) for g in groups for y in range(LINES - distance)]
    held = []
    for k, part in enumerate(slices[:-1]):
        held.append(
            lax.ppermute(
                part,
                "replica",
                [(g + y, g + (y + distance * (k + 1)) % LINES) for g in groups for y in leaving],
            )
        )
    held.append(slices[-1])
    direct = lax.ppermute(value, "replica", near)
    far = []
    for k, part in enumerate(held):
        way = [
            (g + (y + distance * (k + 1)) % LINES, (g + y + distance) % count)
            for g in groups
            for y in leaving
        ]
        far.append(lax.ppermute(part, "replica", way))
    return jnp.where(line < distance, jnp.concatenate(far), direct)


def body(features, cotangent, master, moment, variance, step_count):
    counter = step_count[0]
    selector = counter % 4
    params = master[0]
    tokens = features[0]
    devices = lax.axis_size("fsdp")
    chips = devices // CORES
    half = chips // 2
    index = lax.axis_index("fsdp")
    chip, core = index // CORES, index % CORES
    rows = tokens.shape[0]

    groups = [[at * CORES + c for at in range(chips)] for c in range(CORES)]
    swapped = [(at, at ^ 1) for at in range(devices)]
    mine = params.astype(jnp.bfloat16)
    weights = jnp.concatenate([mine, lax.ppermute(mine, "fsdp", swapped)], axis=1)
    cots = cotangent[0].reshape(rows, chips, CORES * HEAD).transpose(1, 0, 2)

    def pairs_of(step, ways):
        pairs = []
        for core_at, way in enumerate(ways):
            sources = range(step - 1, chips) if way > 0 else range(0, chips - step + 1)
            pairs += [
                (at * CORES + core_at, (at + way) * CORES + core_at)
                for at in sources
                if 0 <= at + way < chips
            ]
        return pairs

    def hop(parts, pairs):
        return [lax.ppermute(part, "fsdp", pairs) for part in parts]

    def exchange(cots, *parts):
        cots, *parts = lax.optimization_barrier((cots, *parts))
        cots = lax.all_to_all(
            cots, "fsdp", split_axis=0, concat_axis=0, axis_index_groups=groups
        )
        return cots, parts

    upper = chip >= half
    parts = jnp.split(tokens, PARTS, axis=0)
    waiting = [(parts, 1, chip)]
    one, two = list(parts), list(parts)
    for step in range(1, half + 1):
        if step == EXCHANGE:
            cots, (one[0], two[0]) = exchange(cots, one[0], two[0])
        one, two = hop(one, pairs_of(step, WAYS)), hop(two, pairs_of(step, [-way for way in WAYS]))
        lead = (core == 0) | (WAYS[0] == WAYS[1])
        if step < half:
            for xs, first in ((list(one), lead), (list(two), ~lead)):
                valid = jnp.where(first, chip >= step, chip < chips - step)
                waiting.append((xs, valid, jnp.where(first, chip - step, chip + step)))
    block = [jnp.where(upper == lead, a, b) for a, b in zip(one, two)]
    for step in range(half, chips):
        if step > half:
            if step == EXCHANGE:
                cots, (block[0],) = exchange(cots, block[0])
            both = sorted(set(pairs_of(step, (1, 1)) + pairs_of(step, (-1, -1))))
            block = hop(block, both)
        valid = jnp.where(upper, chip >= step, chip < chips - step)
        waiting.append((list(block), valid, jnp.where(upper, chip - step, chip + step)))
    sums = tuple(jnp.zeros((D_IN, HEAD), jnp.float32) for _ in range(2))
    for xs, valid, source in waiting:
        sums = accumulate(sums, weights, cots, core, xs, valid, source)
    own, other = sums
    summed = own + lax.ppermute(other, "fsdp", swapped)

    grads = summed * D_IN ** (-0.5)
    power = counter.astype(jnp.float32)
    correct_first = 1.0 - jnp.power(jnp.float32(0.9), power)
    correct_second = 1.0 - jnp.power(jnp.float32(0.999), power)
    first = 0.9 * moment[0].astype(jnp.float32) + 0.1 * grads
    second = 0.999 * variance[0] + 0.001 * grads * grads
    update = 0.1 * (
        first / correct_first / (jnp.sqrt(second / correct_second) + 1e-08) + 0.1 * params
    )
    fresh = params - update
    received = lax.switch(
        selector,
        [partial(pull_fresh, distance=1 << level) for level in range(4)],
        fresh.astype(jnp.bfloat16),
    )
    return (0.5 * (fresh + received.astype(jnp.float32)))[None]


def solution(mesh):
    placed = (
        P("replica", "fsdp", None),
        P("replica", "fsdp", None),
        P("replica", None, "fsdp"),
        P("replica", None, "fsdp"),
        P("replica", None, "fsdp"),
        P(),
    )
    return jax.shard_map(
        body, mesh=mesh, in_specs=placed, out_specs=P("replica", None, "fsdp"), check_vma=False
    )
```
